128 devices in a mesh: aux: 32 (over x, z, core), orb: 4 (over y).
Axes of the slice: x: 4, y: 4, z: 4, core: 2. Of those that a mesh axis runs over, the one named last changes fastest.
Arguments:
- three_centre: bfloat16 [512, 512, 2048], P('orb', 'aux'), may hold values from -6 to 6
- pair_mask: int32 [4, 4], replicated, may hold values 0 or 1
- aux_mask: int32 [4, 16], replicated, may hold values 0 or 1
- density: bfloat16 [512, 1024], P('orb', 'aux'), may hold values from -0.25 to 0.25
Outputs:
- contracted: bfloat16 [2048, 512, 1024], P('aux', 'orb')
The draws below stay inside these ranges and needn't reach their ends.
All inputs are finite; a program needn't handle non-finite values.
Results may differ from the reference program's by a relative error of at most 0.001.
Values may be sent and summed in bfloat16 or wider, within the bound.
No kernel may reach another device: no remote copies, remote signals or barrier semaphores. Data moves between devices by JAX's collectives and lax.ppermute only.
A program may use at most 128 MiB of HBM per device.

```python
import jax
import jax.numpy as jnp
from jax import lax

BLK = 128
NUB = 4
MUB = 4
MU = 512
NU = 512
SIG = 1024
P_SIZE = 2048
PB = 16


def touch_ends(drawn, rng, low, top_value):
    longest = drawn.shape.index(max(drawn.shape))
    spots = []
    for shift in (0, 1):
        where = [jax.random.randint(jax.random.fold_in(rng, axis), (), 0, length) for axis, length in enumerate(drawn.shape)]
        where[longest] = (where[longest] + shift) % drawn.shape[longest]
        spots.append(tuple(where))
    return drawn.at[spots[0]].set(low).at[spots[1]].set(top_value)


def steps_of(key, dims, split, least, top_value):
    def one(axis_at, parts):
        draws = jax.random.uniform(jax.random.fold_in(jax.random.fold_in(key, 6), axis_at), (parts,), jnp.float32, least / len(split), top_value / len(split))
        return jnp.repeat(jnp.exp(draws), dims[axis_at] // parts).reshape((-1,) + (1,) * (len(dims) - axis_at - 1))

    gain = one(*split[0])
    for cut in split[1:]:
        gain = gain * one(*cut)
    return gain


def normal_values(rng, dims, scale, bound, split=(), kind=jnp.bfloat16):
    loudness = steps_of(rng, dims, split, -0.22, 0.18) if split else 1.0
    array = jax.random.normal(rng, dims, jnp.float32) * scale * loudness
    return jnp.minimum(jnp.maximum(array, -bound), bound).astype(kind)


def setup_inputs(seed: int = 0) -> dict:
    splits = jax.random.split(jax.random.key(seed), 5)
    three_centre = normal_values(splits[0], (MU, NU, P_SIZE), 1.0, 6.0, ((0, 4), (1, 32)))
    pair_mask = touch_ends((jax.random.randint(splits[1], (MUB, NUB), 0, 4) < 3).astype(jnp.int32), jax.random.fold_in(splits[1], 1), 0, 1)
    aux_mask = touch_ends((jax.random.randint(splits[2], (NUB, PB), 0, 4) < 3).astype(jnp.int32), jax.random.fold_in(splits[2], 1), 0, 1)
    density = normal_values(splits[3], (NU, SIG), NU ** -0.5, 0.25, ((0, 4), (1, 32)))
    return dict(three_centre=three_centre, pair_mask=pair_mask, aux_mask=aux_mask, density=density)


def reference(three_centre, pair_mask, aux_mask, density):
    pair_full = jnp.repeat(jnp.repeat(pair_mask, BLK, axis=0), BLK, axis=1).astype(jnp.float32)

    def one_block(index):
        start = (index * BLK).astype(jnp.int32)
        slab = lax.dynamic_slice_in_dim(three_centre, start, BLK, 2)
        column = lax.dynamic_slice_in_dim(aux_mask, index.astype(jnp.int32), 1, 1)[:, 0]
        aux_full = jnp.repeat(column, BLK).astype(jnp.float32)
        factor = pair_full[:, :, None] * aux_full[None, :, None]
        masked = (slab.astype(jnp.float32) * factor).astype(jnp.bfloat16)
        rows = jnp.transpose(masked, (2, 0, 1)).reshape(BLK * MU, NU)
        product = jnp.dot(rows, density, preferred_element_type=jnp.float32)
        return product.astype(jnp.bfloat16).reshape(BLK, MU, SIG)

    blocks = lax.map(one_block, jnp.arange(PB, dtype=jnp.int32))
    return blocks.reshape(P_SIZE, MU, SIG)
```

```python
import jax
import jax.numpy as jnp
from jax import lax
from jax.experimental import pallas as pl
from jax.experimental.pallas import tpu as pltpu
from jax.sharding import PartitionSpec as P

BLK = 128
P_STEP = 8


def swap_bit(part, axis, bit):
    count = lax.axis_size(axis)
    other = lax.ppermute(part, axis, [(i, i ^ bit) for i in range(count)])
    upper = (lax.axis_index(axis) & bit) != 0
    return jnp.stack([jnp.where(upper, other, part), jnp.where(upper, part, other)])


def gather_density(density):
    part = density.T
    for axis, bit in (("aux", 8), ("aux", 16), ("aux", 2), ("aux", 4), ("orb", 1), ("orb", 2), ("aux", 1)):
        part = swap_bit(part, axis, bit)
    whole = jnp.transpose(part, (1, 2, 8, 5, 6, 3, 4, 0, 7))
    return whole.reshape(4 * density.shape[0], 32 * density.shape[1])


def contract_kernel(x_ref, d_ref, o_ref):
    sources, step, nu, mu = x_ref.shape
    dens = d_ref[...]
    for p in range(step):
        rows = x_ref[:, p].reshape(sources * nu, mu)
        o_ref[p] = lax.dot_general(
            rows, dens, (((0,), (0,)), ((), ())), preferred_element_type=jnp.float32
        ).astype(jnp.bfloat16)


def contract(moved, dens):
    sources, p_local, nu, mu = moved.shape
    nu_all, sig = dens.shape
    return pl.pallas_call(
        contract_kernel,
        out_shape=jax.ShapeDtypeStruct((p_local, mu, sig), jnp.bfloat16),
        grid=(p_local // P_STEP,),
        in_specs=[
            pl.BlockSpec((sources, P_STEP, nu, mu), lambda i: (0, i, 0, 0)),
            pl.BlockSpec((nu_all, sig), lambda i: (0, 0)),
        ],
        out_specs=pl.BlockSpec((P_STEP, mu, sig), lambda i: (i, 0, 0)),
        compiler_params=pltpu.CompilerParams(vmem_limit_bytes=48 << 20),
        cost_estimate=pl.CostEstimate(
            flops=2 * p_local * mu * nu_all * sig, bytes_accessed=26 << 20, transcendentals=0
        ),
    )(moved, dens)


def local(three_centre, pair_mask, aux_mask, density):
    mu, nu, p_total = three_centre.shape
    aux_pos, orb_pos, aux_count = lax.axis_index("aux"), lax.axis_index("orb"), lax.axis_size("aux")
    p_local = p_total // aux_count
    sent = jnp.transpose(three_centre, (2, 1, 0)).reshape(aux_count, p_local, nu, mu)
    moved = lax.all_to_all(sent, "aux", split_axis=0, concat_axis=0, tiled=True)
    pair = lax.dynamic_index_in_dim(pair_mask, orb_pos, 0, keepdims=False)
    aux = lax.dynamic_index_in_dim(aux_mask, aux_pos * p_local // BLK, 1, keepdims=False)
    keep = jnp.repeat(pair * aux, BLK).astype(jnp.bfloat16)
    dens = gather_density(density) * keep[:, None]
    return contract(moved, dens)


def solution(mesh):
    in_specs = (P("orb", "aux", None), P(), P(), P("orb", "aux"))
    out_specs = P("aux", "orb", None)
    return jax.shard_map(local, mesh=mesh, in_specs=in_specs, out_specs=out_specs, check_vma=False)
```

```python
import jax
import jax.numpy as jnp
from jax import lax
from jax.experimental import pallas as pl
from jax.experimental.pallas import tpu as pltpu
from jax.sharding import PartitionSpec as P

BLK = 128
LANES = 128
HALF = 64
GROUP = 16
PAIRS = 8
PITCH = 24
VMEM = 60 << 20


def swap_bit(part, axis, bit):
    count = lax.axis_size(axis)
    other = lax.ppermute(part, axis, [(i, i ^ bit) for i in range(count)])
    upper = (lax.axis_index(axis) & bit) != 0
    return jnp.stack([jnp.where(upper, other, part), jnp.where(upper, part, other)])


def pack_kernel(x_ref, *rest):
    o_ref = rest[-1]
    for group in range(x_ref.shape[0] // GROUP):
        top = group * GROUP
        for block in range(x_ref.shape[2] // LANES):
            lanes = slice(block * LANES, (block + 1) * LANES)
            low, high = x_ref[top : top + PAIRS, :, lanes], x_ref[top + PAIRS : top + GROUP, :, lanes]
            rows = slice(group * PAIRS, (group + 1) * PAIRS)
            o_ref[2 * block, rows] = jnp.concatenate([low[..., :HALF], high[..., :HALF]], axis=-1)
            o_ref[2 * block + 1, rows] = jnp.concatenate([low[..., HALF:], high[..., HALF:]], axis=-1)


def pack(three_centre, first, count, rows, extra, earlier=None):
    mu, nu, p_total = three_centre.shape
    targets = p_total // HALF
    args, specs, aliases = [three_centre], [pl.BlockSpec((rows, nu, p_total), lambda i: (first + i, 0, 0))], {}
    if earlier is not None:
        args, specs, aliases = args + [earlier], specs + [pl.BlockSpec(memory_space=pl.ANY)], {1: 0}
    return pl.pallas_call(
        pack_kernel,
        out_shape=jax.ShapeDtypeStruct((targets, mu // 2 + extra, nu, LANES), jnp.bfloat16),
        grid=(count,),
        in_specs=specs,
        out_specs=pl.BlockSpec((targets, rows // 2, nu, LANES), lambda i: (0, first + i, 0, 0)),
        input_output_aliases=aliases,
        compiler_params=pltpu.CompilerParams(vmem_limit_bytes=VMEM),
        cost_estimate=pl.CostEstimate(
            flops=0, bytes_accessed=4 * count * rows * nu * p_total, transcendentals=0
        ),
    )(*args)


def append_kernel(d_ref, sent_ref, o_ref):
    half = d_ref.shape[1] // 2
    for target in range(o_ref.shape[0]):
        core = target % 2
        o_ref[target] = d_ref[:, core * half : (core + 1) * half]


def append(sent, columns):
    targets, rows, nu, lanes = sent.shape
    orbs = columns.shape[0]
    return pl.pallas_call(
        append_kernel,
        out_shape=jax.ShapeDtypeStruct(sent.shape, sent.dtype),
        grid=(1,),
        in_specs=[pl.BlockSpec(columns.shape, lambda i: (0, 0, 0)), pl.BlockSpec(memory_space=pl.ANY)],
        out_specs=pl.BlockSpec((targets, orbs, nu, lanes), lambda i: (0, rows // orbs - 1, 0, 0)),
        input_output_aliases={1: 0},
        compiler_params=pltpu.CompilerParams(vmem_limit_bytes=VMEM),
    )(columns, sent)


def contract_kernel(keep_ref, x_ref, mine_ref, other_ref, o_ref, dens_ref, rows_ref):
    sources, _, nu, _ = x_ref.shape
    depth = sources * nu
    _, orbs, half, lanes = mine_ref.shape

    @pl.when(pl.program_id(0) == 0)
    def _():
        upper = keep_ref[orbs] == 1
        for orb in range(orbs):
            keep = keep_ref[orb].astype(jnp.float32).astype(jnp.bfloat16)
            mine, other = mine_ref[:, orb], other_ref[:, orb]
            low, high = jnp.where(upper, other, mine), jnp.where(upper, mine, other)
            whole = jnp.stack([low, high], axis=1).reshape(sources * 2 * half, lanes)
            dens_ref[orb * lanes : (orb + 1) * lanes, :] = whole.T * keep

    for pair in range(PAIRS):
        turned = x_ref[:, pair].reshape(depth, LANES).T.astype(jnp.float32)
        for k in range(depth // LANES):
            piece = turned[:, k * LANES : (k + 1) * LANES]
            base = k * HALF * PITCH + pair
            rows_ref[pl.ds(base, HALF, stride=PITCH), :] = piece[:HALF]
            rows_ref[pl.ds(base + PAIRS, HALF, stride=PITCH), :] = piece[HALF:]
    pieces = []
    for k in range(depth // LANES):
        piece = rows_ref[k * HALF * PITCH : (k + 1) * HALF * PITCH, :].reshape(HALF, PITCH, LANES)
        pieces.append(piece[:, :GROUP].reshape(HALF * GROUP, LANES).astype(jnp.bfloat16))
    product = jnp.dot(jnp.concatenate(pieces, axis=1), dens_ref[...], preferred_element_type=jnp.float32)
    o_ref[...] = product.astype(jnp.bfloat16).reshape(o_ref.shape)


def contract(moved, other, keep):
    sources, orbs, nu, _ = other.shape
    pairs = moved.shape[1] - orbs
    sig = sources * 2 * nu
    return pl.pallas_call(
        contract_kernel,
        out_shape=jax.ShapeDtypeStruct((HALF, 2 * pairs, sig), jnp.bfloat16),
        grid=(pairs // PAIRS,),
        in_specs=[
            pl.BlockSpec(memory_space=pltpu.SMEM),
            pl.BlockSpec((sources, PAIRS, nu, LANES), lambda i: (0, i, 0, 0)),
            pl.BlockSpec((sources, orbs, nu, LANES), lambda i: (0, pairs // orbs, 0, 0)),
            pl.BlockSpec(other.shape, lambda i: (0, 0, 0, 0)),
        ],
        out_specs=pl.BlockSpec((HALF, GROUP, sig), lambda i: (0, i, 0)),
        scratch_shapes=[
            pltpu.VMEM((orbs * LANES, sig), jnp.bfloat16),
            pltpu.VMEM((orbs * HALF * PITCH, LANES), jnp.float32),
        ],
        compiler_params=pltpu.CompilerParams(vmem_limit_bytes=VMEM),
        cost_estimate=pl.CostEstimate(
            flops=4 * HALF * pairs * orbs * LANES * sig, bytes_accessed=26 << 20, transcendentals=0
        ),
    )(keep, moved, moved, other)


def local(three_centre, pair_mask, aux_mask, density):
    mu, nu, p_total = three_centre.shape
    aux_pos, orb_pos, aux_count = lax.axis_index("aux"), lax.axis_index("orb"), lax.axis_size("aux")
    orbs = lax.axis_size("orb")
    pair = lax.dynamic_index_in_dim(pair_mask, orb_pos, 0, keepdims=False)
    aux = lax.dynamic_index_in_dim(aux_mask, aux_pos * (p_total // aux_count) // BLK, 1, keepdims=False)
    keep = jnp.concatenate([pair * aux, jnp.full((1,), aux_pos % 2, jnp.int32)])

    part = swap_bit(density.T, "orb", 1)
    sent = pack(three_centre, 0, mu // 64, 32, orbs)
    part, sent = lax.optimization_barrier((part, sent))
    columns = swap_bit(part, "orb", 2).reshape(orbs, density.shape[1], density.shape[0])
    sent = pack(three_centre, mu // 64, mu // 64, 32, orbs, sent)
    sent = append(sent, columns)
    sent, keep = lax.optimization_barrier((sent, keep))
    moved = lax.all_to_all(sent, "aux", split_axis=0, concat_axis=0, tiled=True)
    other = lax.ppermute(moved[:, mu // 2 :], "aux", [(i, i ^ 1) for i in range(aux_count)])
    return contract(moved, other, keep)


def solution(mesh):
    in_specs = (P("orb", "aux", None), P(), P(), P("orb", "aux"))
    out_specs = P("aux", "orb", None)
    return jax.shard_map(local, mesh=mesh, in_specs=in_specs, out_specs=out_specs, check_vma=False)
```

```python
import jax
import jax.numpy as jnp
from jax import lax
from jax.experimental import pallas as pl
from jax.experimental.pallas import tpu as pltpu
from jax.sharding import PartitionSpec as P

BLK = 128
LANES = 128
HALF = 64
GROUP = 16
PAIRS = 8
SUBS = 2
PITCH = 24
VMEM = 60 << 20


def pack_kernel(x_ref, *rest):
    o_ref = rest[-1]
    for group in range(x_ref.shape[0] // GROUP):
        top = group * GROUP
        for block in range(x_ref.shape[2] // LANES):
            lanes = slice(block * LANES, (block + 1) * LANES)
            low, high = x_ref[top : top + PAIRS, :, lanes], x_ref[top + PAIRS : top + GROUP, :, lanes]
            rows = slice(group * PAIRS, (group + 1) * PAIRS)
            o_ref[2 * block, rows] = jnp.concatenate([low[..., :HALF], high[..., :HALF]], axis=-1)
            o_ref[2 * block + 1, rows] = jnp.concatenate([low[..., HALF:], high[..., HALF:]], axis=-1)


def pack(three_centre, first, count, rows, extra, earlier=None):
    mu, nu, p_total = three_centre.shape
    targets = p_total // HALF
    args, specs, aliases = [three_centre], [pl.BlockSpec((rows, nu, p_total), lambda i: (first + i, 0, 0))], {}
    if earlier is not None:
        args, specs, aliases = args + [earlier], specs + [pl.BlockSpec(memory_space=pl.ANY)], {1: 0}
    return pl.pallas_call(
        pack_kernel,
        out_shape=jax.ShapeDtypeStruct((targets, mu // 2 + extra, nu, LANES), jnp.bfloat16),
        grid=(count,),
        in_specs=specs,
        out_specs=pl.BlockSpec((targets, rows // 2, nu, LANES), lambda i: (0, first + i, 0, 0)),
        input_output_aliases=aliases,
        compiler_params=pltpu.CompilerParams(vmem_limit_bytes=VMEM),
        cost_estimate=pl.CostEstimate(
            flops=0, bytes_accessed=4 * count * rows * nu * p_total, transcendentals=0
        ),
    )(*args)


def append_kernel(*refs):
    o_ref, parts = refs[-1], refs[:-2]
    half = parts[0].shape[0] // 2
    for step, part in zip((0, -1, 1, 2), parts):
        orb = lax.rem(lax.axis_index("orb") + len(parts) + step, len(parts))
        for target in range(o_ref.shape[0]):
            core = target % 2
            o_ref[target, orb] = part[core * half : (core + 1) * half, :]


def append(sent, parts):
    targets, rows, nu, lanes = sent.shape
    orbs = len(parts)
    return pl.pallas_call(
        append_kernel,
        out_shape=jax.ShapeDtypeStruct(sent.shape, sent.dtype),
        grid=(1,),
        in_specs=[pl.BlockSpec(part.shape, lambda i: (0, 0)) for part in parts]
        + [pl.BlockSpec(memory_space=pl.ANY)],
        out_specs=pl.BlockSpec((targets, orbs, nu, lanes), lambda i: (0, rows // orbs - 1, 0, 0)),
        input_output_aliases={orbs: 0},
        compiler_params=pltpu.CompilerParams(vmem_limit_bytes=50 << 20),
    )(*parts, sent)


def contract_kernel(pair_ref, aux_ref, x_ref, mine_ref, other_ref, o_ref, dens_ref, rows_ref):
    sources, _, nu, _ = x_ref.shape
    depth = sources * nu
    _, orbs, half, lanes = mine_ref.shape
    aux_pos, orb_pos = lax.axis_index("aux"), lax.axis_index("orb")

    @pl.when(pl.program_id(0) == 0)
    def _():
        upper = lax.rem(aux_pos, 2) == 1
        column = lax.div(aux_pos * HALF, BLK)
        for orb in range(orbs):
            keep = (pair_ref[orb_pos, orb] * aux_ref[orb, column]).astype(jnp.float32).astype(jnp.bfloat16)
            mine, other = mine_ref[:, orb], other_ref[:, orb]
            low, high = jnp.where(upper, other, mine), jnp.where(upper, mine, other)
            whole = jnp.stack([low, high], axis=1).reshape(sources * 2 * half, lanes)
            dens_ref[orb * lanes : (orb + 1) * lanes, :] = whole.T * keep

    def order_rows(sub, pair):
        turned = x_ref[:, sub * PAIRS + pair].reshape(depth, LANES).T.astype(jnp.float32)
        for k in range(depth // LANES):
            piece = turned[:, k * LANES : (k + 1) * LANES]
            base = k * HALF * PITCH + pair
            rows_ref[sub, pl.ds(base, HALF, stride=PITCH), :] = piece[:HALF]
            rows_ref[sub, pl.ds(base + PAIRS, HALF, stride=PITCH), :] = piece[HALF:]

    def multiply(sub):
        pieces = []
        for k in range(depth // LANES):
            piece = rows_ref[sub, k * HALF * PITCH : (k + 1) * HALF * PITCH, :].reshape(HALF, PITCH, LANES)
            pieces.append(piece[:, :GROUP].reshape(HALF * GROUP, LANES).astype(jnp.bfloat16))
        product = jnp.dot(jnp.concatenate(pieces, axis=1), dens_ref[...], preferred_element_type=jnp.float32)
        mus = slice(sub * GROUP, (sub + 1) * GROUP)
        o_ref[:, mus] = product.astype(jnp.bfloat16).reshape(HALF, GROUP, -1)

    for sub in range(SUBS):
        for pair in range(PAIRS):
            order_rows(sub, pair)
    for sub in range(SUBS):
        multiply(sub)


def contract(moved, other, pair_mask, aux_mask):
    sources, orbs, nu, _ = other.shape
    pairs = moved.shape[1] - orbs
    sig = sources * 2 * nu
    return pl.pallas_call(
        contract_kernel,
        out_shape=jax.ShapeDtypeStruct((HALF, 2 * pairs, sig), jnp.bfloat16),
        grid=(pairs // (SUBS * PAIRS),),
        in_specs=[
            pl.BlockSpec(memory_space=pltpu.SMEM),
            pl.BlockSpec(memory_space=pltpu.SMEM),
            pl.BlockSpec((sources, SUBS * PAIRS, nu, LANES), lambda i: (0, i, 0, 0)),
            pl.BlockSpec((sources, orbs, nu, LANES), lambda i: (0, pairs // orbs, 0, 0)),
            pl.BlockSpec(other.shape, lambda i: (0, 0, 0, 0)),
        ],
        out_specs=pl.BlockSpec((HALF, SUBS * GROUP, sig), lambda i: (0, i, 0)),
        scratch_shapes=[
            pltpu.VMEM((orbs * LANES, sig), jnp.bfloat16),
            pltpu.VMEM((SUBS, orbs * HALF * PITCH, LANES), jnp.float32),
        ],
        compiler_params=pltpu.CompilerParams(vmem_limit_bytes=36 << 20),
        cost_estimate=pl.CostEstimate(
            flops=4 * HALF * pairs * orbs * LANES * sig, bytes_accessed=26 << 20, transcendentals=0
        ),
    )(pair_mask, aux_mask, moved, moved, other)


def local(three_centre, pair_mask, aux_mask, density):
    mu, nu, p_total = three_centre.shape
    aux_count, orbs = lax.axis_size("aux"), lax.axis_size("orb")
    own = density.T
    up, down = [(i, (i + 1) % orbs) for i in range(orbs)], [(i, (i - 1) % orbs) for i in range(orbs)]
    before = lax.ppermute(own, "orb", up)
    after = lax.ppermute(own, "orb", down)
    sent = pack(three_centre, 0, mu // 64, 32, orbs)
    before, after, sent = lax.optimization_barrier((before, after, sent))
    across = lax.ppermute(before, "orb", up)
    sent = pack(three_centre, mu // 64, mu // 64, 32, orbs, sent)
    sent = append(sent, (own, before, after, across))
    moved = lax.all_to_all(sent, "aux", split_axis=0, concat_axis=0, tiled=True)
    other = lax.ppermute(moved[:, mu // 2 :], "aux", [(i, i ^ 1) for i in range(aux_count)])
    return contract(moved, other, pair_mask, aux_mask)


def solution(mesh):
    in_specs = (P("orb", "aux", None), P(), P(), P("orb", "aux"))
    out_specs = P("aux", "orb", None)
    return jax.shard_map(local, mesh=mesh, in_specs=in_specs, out_specs=out_specs, check_vma=False)
```

```python
import jax
import jax.numpy as jnp
from jax import lax
from jax.experimental import pallas as pl
from jax.experimental.pallas import tpu as pltpu
from jax.sharding import PartitionSpec as P

BLK = 128
LANES = 128
HALF = 64
GROUP = 16
PAIRS = 8
SUBS = 2
PITCH = 24
VMEM = 60 << 20


def pack_kernel(x_ref, *rest):
    o_ref = rest[-1]
    for group in range(x_ref.shape[0] // GROUP):
        top = group * GROUP
        for block in range(x_ref.shape[2] // LANES):
            lanes = slice(block * LANES, (block + 1) * LANES)
            low, high = x_ref[top : top + PAIRS, :, lanes], x_ref[top + PAIRS : top + GROUP, :, lanes]
            rows = slice(group * PAIRS, (group + 1) * PAIRS)
            o_ref[2 * block, rows] = jnp.concatenate([low[..., :HALF], high[..., :HALF]], axis=-1)
            o_ref[2 * block + 1, rows] = jnp.concatenate([low[..., HALF:], high[..., HALF:]], axis=-1)


def pack(three_centre, first, count, rows, extra, earlier=None):
    mu, nu, p_total = three_centre.shape
    targets = p_total // HALF
    args, specs, aliases = [pltpu.with_memory_space_constraint(three_centre, pltpu.HBM)], [pl.BlockSpec((rows, nu, p_total), lambda i: (first + i, 0, 0))], {}
    if earlier is not None:
        args, specs, aliases = args + [earlier], specs + [pl.BlockSpec(memory_space=pl.ANY)], {1: 0}
    return pl.pallas_call(
        pack_kernel,
        out_shape=jax.ShapeDtypeStruct((targets, mu // 2 + extra, nu, LANES), jnp.bfloat16),
        grid=(count,),
        in_specs=specs,
        out_specs=pl.BlockSpec((targets, rows // 2, nu, LANES), lambda i: (0, first + i, 0, 0)),
        input_output_aliases=aliases,
        compiler_params=pltpu.CompilerParams(vmem_limit_bytes=28 << 20),
        cost_estimate=pl.CostEstimate(
            flops=0, bytes_accessed=4 * count * rows * nu * p_total, transcendentals=0
        ),
    )(*args)


def append_kernel(*refs):
    o_ref, parts = refs[-1], refs[:-2]
    half = parts[0].shape[0] // 2
    for step, part in zip((0, -1, 1, 2), parts):
        orb = lax.rem(lax.axis_index("orb") + len(parts) + step, len(parts))
        for target in range(o_ref.shape[0]):
            core = target % 2
            o_ref[target, orb] = part[core * half : (core + 1) * half, :]


def append(sent, parts):
    targets, rows, nu, lanes = sent.shape
    orbs = len(parts)
    return pl.pallas_call(
        append_kernel,
        out_shape=jax.ShapeDtypeStruct(sent.shape, sent.dtype),
        grid=(1,),
        in_specs=[pl.BlockSpec(part.shape, lambda i: (0, 0)) for part in parts]
        + [pl.BlockSpec(memory_space=pl.ANY)],
        out_specs=pl.BlockSpec((targets, orbs, nu, lanes), lambda i: (0, rows // orbs - 1, 0, 0)),
        input_output_aliases={orbs: 0},
        compiler_params=pltpu.CompilerParams(vmem_limit_bytes=28 << 20),
    )(*parts, sent)


def contract_kernel(pair_ref, aux_ref, x_ref, mine_ref, other_ref, o_ref, dens_ref, rows_ref):
    sources, _, nu, _ = x_ref.shape
    depth = sources * nu
    _, orbs, half, lanes = mine_ref.shape
    aux_pos, orb_pos = lax.axis_index("aux"), lax.axis_index("orb")

    @pl.when(pl.program_id(0) == 0)
    def _():
        upper = lax.rem(aux_pos, 2) == 1
        column = lax.div(aux_pos * HALF, BLK)
        for orb in range(orbs):
            keep = (pair_ref[orb_pos, orb] * aux_ref[orb, column]).astype(jnp.float32).astype(jnp.bfloat16)
            mine, other = mine_ref[:, orb], other_ref[:, orb]
            low, high = jnp.where(upper, other, mine), jnp.where(upper, mine, other)
            whole = jnp.stack([low, high], axis=1).reshape(sources * 2 * half, lanes)
            dens_ref[orb * lanes : (orb + 1) * lanes, :] = whole.T * keep

    def order_rows(sub, pair):
        turned = x_ref[:, sub * PAIRS + pair].reshape(depth, LANES).T.astype(jnp.float32)
        for k in range(depth // LANES):
            piece = turned[:, k * LANES : (k + 1) * LANES]
            base = k * HALF * PITCH + pair
            rows_ref[sub, pl.ds(base, HALF, stride=PITCH), :] = piece[:HALF]
            rows_ref[sub, pl.ds(base + PAIRS, HALF, stride=PITCH), :] = piece[HALF:]

    def multiply(sub):
        pieces = []
        for k in range(depth // LANES):
            piece = rows_ref[sub, k * HALF * PITCH : (k + 1) * HALF * PITCH, :].reshape(HALF, PITCH, LANES)
            pieces.append(piece[:, :GROUP].reshape(HALF * GROUP, LANES).astype(jnp.bfloat16))
        product = jnp.dot(jnp.concatenate(pieces, axis=1), dens_ref[...], preferred_element_type=jnp.float32)
        mus = slice(sub * GROUP, (sub + 1) * GROUP)
        o_ref[:, mus] = product.astype(jnp.bfloat16).reshape(HALF, GROUP, -1)

    for sub in range(SUBS):
        for pair in range(PAIRS):
            order_rows(sub, pair)
    for sub in range(SUBS):
        multiply(sub)


def contract(moved, other, pair_mask, aux_mask):
    sources, orbs, nu, _ = other.shape
    pairs = moved.shape[1] - orbs
    sig = sources * 2 * nu
    return pl.pallas_call(
        contract_kernel,
        out_shape=jax.ShapeDtypeStruct((HALF, 2 * pairs, sig), jnp.bfloat16),
        grid=(pairs // (SUBS * PAIRS),),
        in_specs=[
            pl.BlockSpec(memory_space=pltpu.SMEM),
            pl.BlockSpec(memory_space=pltpu.SMEM),
            pl.BlockSpec((sources, SUBS * PAIRS, nu, LANES), lambda i: (0, i, 0, 0)),
            pl.BlockSpec((sources, orbs, nu, LANES), lambda i: (0, pairs // orbs, 0, 0)),
            pl.BlockSpec(other.shape, lambda i: (0, 0, 0, 0)),
        ],
        out_specs=pl.BlockSpec((HALF, SUBS * GROUP, sig), lambda i: (0, i, 0)),
        scratch_shapes=[
            pltpu.VMEM((orbs * LANES, sig), jnp.bfloat16),
            pltpu.VMEM((SUBS, orbs * HALF * PITCH, LANES), jnp.float32),
        ],
        compiler_params=pltpu.CompilerParams(vmem_limit_bytes=36 << 20),
        cost_estimate=pl.CostEstimate(
            flops=4 * HALF * pairs * orbs * LANES * sig, bytes_accessed=26 << 20, transcendentals=0
        ),
    )(pair_mask, aux_mask, moved, moved, other)


def local(three_centre, pair_mask, aux_mask, density):
    mu, nu, p_total = three_centre.shape
    aux_count, orbs = lax.axis_size("aux"), lax.axis_size("orb")
    own = density.T
    up, down = [(i, (i + 1) % orbs) for i in range(orbs)], [(i, (i - 1) % orbs) for i in range(orbs)]
    two_up = [(i, (i + 2) % orbs) for i in range(orbs)]
    before, after, across = (lax.ppermute(own, "orb", pairs) for pairs in (up, down, two_up))
    sent = pack(three_centre, 0, mu // 32, 32, orbs)
    sent = append(sent, (own, before, after, across))
    moved = lax.all_to_all(sent, "aux", split_axis=0, concat_axis=0, tiled=True)
    other = lax.ppermute(moved[:, mu // 2 :], "aux", [(i, i ^ 1) for i in range(aux_count)])
    return contract(moved, other, pair_mask, aux_mask)


def solution(mesh):
    in_specs = (P("orb", "aux", None), P(), P(), P("orb", "aux"))
    out_specs = P("aux", "orb", None)
    return jax.shard_map(local, mesh=mesh, in_specs=in_specs, out_specs=out_specs, check_vma=False)
```

```python
import jax
import jax.numpy as jnp
from jax import lax
from jax.experimental import pallas as pl
from jax.experimental.pallas import tpu as pltpu
from jax.sharding import PartitionSpec as P

BLK = 128
LANES = 128
HALF = 64
GROUP = 16
PAIRS = 8
SUBS = 2
PITCH = 24
VMEM = 60 << 20


def pack_kernel(x_ref, *rest):
    o_ref = rest[-1]
    for group in range(x_ref.shape[0] // GROUP):
        top = group * GROUP
        for block in range(x_ref.shape[2] // LANES):
            lanes = slice(block * LANES, (block + 1) * LANES)
            low, high = x_ref[top : top + PAIRS, :, lanes], x_ref[top + PAIRS : top + GROUP, :, lanes]
            rows = slice(group * PAIRS, (group + 1) * PAIRS)
            o_ref[2 * block, rows] = jnp.concatenate([low[..., :HALF], high[..., :HALF]], axis=-1)
            o_ref[2 * block + 1, rows] = jnp.concatenate([low[..., HALF:], high[..., HALF:]], axis=-1)


def pack(three_centre, first, count, rows, extra, earlier=None):
    mu, nu, p_total = three_centre.shape
    targets = p_total // HALF
    args, specs, aliases = [pltpu.with_memory_space_constraint(three_centre, pltpu.HBM)], [pl.BlockSpec((rows, nu, p_total), lambda i: (first + i, 0, 0))], {}
    if earlier is not None:
        args, specs, aliases = args + [earlier], specs + [pl.BlockSpec(memory_space=pl.ANY)], {1: 0}
    return pl.pallas_call(
        pack_kernel,
        out_shape=jax.ShapeDtypeStruct((targets, mu // 2 + extra, nu, LANES), jnp.bfloat16),
        grid=(count,),
        in_specs=specs,
        out_specs=pl.BlockSpec((targets, rows // 2, nu, LANES), lambda i: (0, first + i, 0, 0)),
        input_output_aliases=aliases,
        compiler_params=pltpu.CompilerParams(vmem_limit_bytes=36 << 20),
        cost_estimate=pl.CostEstimate(
            flops=0, bytes_accessed=4 * count * rows * nu * p_total, transcendentals=0
        ),
    )(*args)


def append_kernel(*refs):
    o_ref, parts = refs[-1], refs[:-2]
    half = parts[0].shape[0] // 2
    for step, part in enumerate(parts):
        orb = lax.axis_index("orb") ^ step
        for target in range(o_ref.shape[0]):
            core = target % 2
            o_ref[target, orb] = part[core * half : (core + 1) * half, :]


def append(sent, parts):
    targets, rows, nu, lanes = sent.shape
    orbs = len(parts)
    return pl.pallas_call(
        append_kernel,
        out_shape=jax.ShapeDtypeStruct(sent.shape, sent.dtype),
        grid=(1,),
        in_specs=[pl.BlockSpec(part.shape, lambda i: (0, 0)) for part in parts]
        + [pl.BlockSpec(memory_space=pl.ANY)],
        out_specs=pl.BlockSpec((targets, orbs, nu, lanes), lambda i: (0, rows // orbs - 1, 0, 0)),
        input_output_aliases={orbs: 0},
        compiler_params=pltpu.CompilerParams(vmem_limit_bytes=36 << 20),
    )(*parts, sent)


def contract_kernel(pair_ref, aux_ref, x_ref, mine_ref, other_ref, o_ref, dens_ref, rows_ref):
    sources, _, nu, _ = x_ref.shape
    depth = sources * nu
    _, orbs, half, lanes = mine_ref.shape
    aux_pos, orb_pos = lax.axis_index("aux"), lax.axis_index("orb")

    @pl.when(pl.program_id(0) == 0)
    def _():
        upper = lax.rem(aux_pos, 2) == 1
        column = lax.div(aux_pos * HALF, BLK)
        for orb in range(orbs):
            keep = (pair_ref[orb_pos, orb] * aux_ref[orb, column]).astype(jnp.float32).astype(jnp.bfloat16)
            mine, other = mine_ref[:, orb], other_ref[:, orb]
            low, high = jnp.where(upper, other, mine), jnp.where(upper, mine, other)
            whole = jnp.stack([low, high], axis=1).reshape(sources * 2 * half, lanes)
            dens_ref[orb * lanes : (orb + 1) * lanes, :] = whole.T * keep

    def order_rows(sub, pair):
        turned = x_ref[:, sub * PAIRS + pair].reshape(depth, LANES).T.astype(jnp.float32)
        for k in range(depth // LANES):
            piece = turned[:, k * LANES : (k + 1) * LANES]
            base = k * HALF * PITCH + pair
            rows_ref[sub, pl.ds(base, HALF, stride=PITCH), :] = piece[:HALF]
            rows_ref[sub, pl.ds(base + PAIRS, HALF, stride=PITCH), :] = piece[HALF:]

    def multiply(sub):
        pieces = []
        for k in range(depth // LANES):
            piece = rows_ref[sub, k * HALF * PITCH : (k + 1) * HALF * PITCH, :].reshape(HALF, PITCH, LANES)
            pieces.append(piece[:, :GROUP].reshape(HALF * GROUP, LANES).astype(jnp.bfloat16))
        product = jnp.dot(jnp.concatenate(pieces, axis=1), dens_ref[...], preferred_element_type=jnp.float32)
        mus = slice(sub * GROUP, (sub + 1) * GROUP)
        o_ref[:, mus] = product.astype(jnp.bfloat16).reshape(HALF, GROUP, -1)

    for sub in range(SUBS):
        for pair in range(PAIRS):
            order_rows(sub, pair)
    for sub in range(SUBS):
        multiply(sub)


def contract(moved, other, pair_mask, aux_mask):
    sources, orbs, nu, _ = other.shape
    pairs = moved.shape[1] - orbs
    sig = sources * 2 * nu
    return pl.pallas_call(
        contract_kernel,
        out_shape=jax.ShapeDtypeStruct((HALF, 2 * pairs, sig), jnp.bfloat16),
        grid=(pairs // (SUBS * PAIRS),),
        in_specs=[
            pl.BlockSpec(memory_space=pltpu.SMEM),
            pl.BlockSpec(memory_space=pltpu.SMEM),
            pl.BlockSpec((sources, SUBS * PAIRS, nu, LANES), lambda i: (0, i, 0, 0)),
            pl.BlockSpec((sources, orbs, nu, LANES), lambda i: (0, pairs // orbs, 0, 0)),
            pl.BlockSpec(other.shape, lambda i: (0, 0, 0, 0)),
        ],
        out_specs=pl.BlockSpec((HALF, SUBS * GROUP, sig), lambda i: (0, i, 0)),
        scratch_shapes=[
            pltpu.VMEM((orbs * LANES, sig), jnp.bfloat16),
            pltpu.VMEM((SUBS, orbs * HALF * PITCH, LANES), jnp.float32),
        ],
        compiler_params=pltpu.CompilerParams(vmem_limit_bytes=36 << 20),
        cost_estimate=pl.CostEstimate(
            flops=4 * HALF * pairs * orbs * LANES * sig, bytes_accessed=26 << 20, transcendentals=0
        ),
    )(pair_mask, aux_mask, moved, moved, other)


def local(three_centre, pair_mask, aux_mask, density):
    mu, nu, p_total = three_centre.shape
    aux_count, orbs = lax.axis_size("aux"), lax.axis_size("orb")
    own = density.T
    others = [lax.ppermute(own, "orb", [(i, i ^ step) for i in range(orbs)]) for step in range(1, orbs)]
    sent = pack(three_centre, 0, mu // 64, 64, orbs)
    sent = append(sent, (own, *others))
    moved = lax.all_to_all(sent, "aux", split_axis=0, concat_axis=0, tiled=True)
    other = lax.ppermute(moved[:, mu // 2 :], "aux", [(i, i ^ 1) for i in range(aux_count)])
    return contract(moved, other, pair_mask, aux_mask)


def solution(mesh):
    in_specs = (P("orb", "aux", None), P(), P(), P("orb", "aux"))
    out_specs = P("aux", "orb", None)
    return jax.shard_map(local, mesh=mesh, in_specs=in_specs, out_specs=out_specs, check_vma=False)
```

```python
import jax
import jax.numpy as jnp
from jax import lax
from jax.experimental import pallas as pl
from jax.experimental.pallas import tpu as pltpu
from jax.sharding import PartitionSpec as P

BLK = 128
LANES = 128
HALF = 64
GROUP = 16
PAIRS = 8
SUBS = 2
PITCH = 24


def pack_kernel(x_ref, o_ref, held_ref, sems):
    groups = x_ref.shape[0] // GROUP

    def fetch(group):
        rows = pl.ds(group * GROUP, GROUP)
        return pltpu.make_async_copy(x_ref.at[rows], held_ref.at[rows], sems.at[group])

    for group in range(groups):
        fetch(group).start()
    for group in range(groups):
        fetch(group).wait()
        top = group * GROUP
        for block in range(x_ref.shape[2] // LANES):
            lanes = slice(block * LANES, (block + 1) * LANES)
            low, high = held_ref[top : top + PAIRS, :, lanes], held_ref[top + PAIRS : top + GROUP, :, lanes]
            rows = slice(group * PAIRS, (group + 1) * PAIRS)
            o_ref[2 * block, rows] = jnp.concatenate([low[..., :HALF], high[..., :HALF]], axis=-1)
            o_ref[2 * block + 1, rows] = jnp.concatenate([low[..., HALF:], high[..., HALF:]], axis=-1)


def pack(three_centre, extra):
    mu, nu, p_total = three_centre.shape
    return pl.pallas_call(
        pack_kernel,
        out_shape=pltpu.VMEM((p_total // HALF, mu // 2 + extra, nu, LANES), jnp.bfloat16),
        in_specs=[pl.BlockSpec(memory_space=pl.ANY)],
        out_specs=pl.BlockSpec(memory_space=pltpu.VMEM),
        scratch_shapes=[pltpu.VMEM(three_centre.shape, jnp.bfloat16), pltpu.SemaphoreType.DMA((mu // GROUP,))],
        compiler_params=pltpu.CompilerParams(vmem_limit_bytes=36 << 20),
        cost_estimate=pl.CostEstimate(flops=0, bytes_accessed=4 * mu * nu * p_total, transcendentals=0),
    )(pltpu.with_memory_space_constraint(three_centre, pltpu.HBM))


def append_kernel(*refs):
    o_ref, parts = refs[-1], refs[:-2]
    half = parts[0].shape[0] // 2
    for step, part in enumerate(parts):
        orb = lax.axis_index("orb") ^ step
        for target in range(o_ref.shape[0]):
            core = target % 2
            o_ref[target, orb] = part[core * half : (core + 1) * half, :]


def append(sent, parts):
    targets, rows, nu, lanes = sent.shape
    orbs = len(parts)
    return pl.pallas_call(
        append_kernel,
        out_shape=jax.ShapeDtypeStruct(sent.shape, sent.dtype),
        grid=(1,),
        in_specs=[pl.BlockSpec(part.shape, lambda i: (0, 0)) for part in parts]
        + [pl.BlockSpec(memory_space=pl.ANY)],
        out_specs=pl.BlockSpec((targets, orbs, nu, lanes), lambda i: (0, rows // orbs - 1, 0, 0)),
        input_output_aliases={orbs: 0},
        compiler_params=pltpu.CompilerParams(vmem_limit_bytes=36 << 20),
    )(*parts, sent)


def contract_kernel(pair_ref, aux_ref, x_ref, mine_ref, other_ref, o_ref, dens_ref, rows_ref):
    sources, _, nu, _ = x_ref.shape
    depth = sources * nu
    _, orbs, half, lanes = mine_ref.shape
    aux_pos, orb_pos = lax.axis_index("aux"), lax.axis_index("orb")

    @pl.when(pl.program_id(0) == 0)
    def _():
        upper = lax.rem(aux_pos, 2) == 1
        column = lax.div(aux_pos * HALF, BLK)
        for orb in range(orbs):
            keep = (pair_ref[orb_pos, orb] * aux_ref[orb, column]).astype(jnp.float32).astype(jnp.bfloat16)
            mine, other = mine_ref[:, orb], other_ref[:, orb]
            low, high = jnp.where(upper, other, mine), jnp.where(upper, mine, other)
            whole = jnp.stack([low, high], axis=1).reshape(sources * 2 * half, lanes)
            dens_ref[orb * lanes : (orb + 1) * lanes, :] = whole.T * keep

    def order_rows(sub, pair):
        turned = x_ref[:, sub * PAIRS + pair].reshape(depth, LANES).T.astype(jnp.float32)
        for k in range(depth // LANES):
            piece = turned[:, k * LANES : (k + 1) * LANES]
            base = k * HALF * PITCH + pair
            rows_ref[sub, pl.ds(base, HALF, stride=PITCH), :] = piece[:HALF]
            rows_ref[sub, pl.ds(base + PAIRS, HALF, stride=PITCH), :] = piece[HALF:]

    def multiply(sub):
        pieces = []
        for k in range(depth // LANES):
            piece = rows_ref[sub, k * HALF * PITCH : (k + 1) * HALF * PITCH, :].reshape(HALF, PITCH, LANES)
            pieces.append(piece[:, :GROUP].reshape(HALF * GROUP, LANES).astype(jnp.bfloat16))
        product = jnp.dot(jnp.concatenate(pieces, axis=1), dens_ref[...], preferred_element_type=jnp.float32)
        mus = slice(sub * GROUP, (sub + 1) * GROUP)
        o_ref[:, mus] = product.astype(jnp.bfloat16).reshape(HALF, GROUP, -1)

    for sub in range(SUBS):
        for pair in range(PAIRS):
            order_rows(sub, pair)
    for sub in range(SUBS):
        multiply(sub)


def contract(moved, other, pair_mask, aux_mask):
    sources, orbs, nu, _ = other.shape
    pairs = moved.shape[1] - orbs
    sig = sources * 2 * nu
    return pl.pallas_call(
        contract_kernel,
        out_shape=jax.ShapeDtypeStruct((HALF, 2 * pairs, sig), jnp.bfloat16),
        grid=(pairs // (SUBS * PAIRS),),
        in_specs=[
            pl.BlockSpec(memory_space=pltpu.SMEM),
            pl.BlockSpec(memory_space=pltpu.SMEM),
            pl.BlockSpec((sources, SUBS * PAIRS, nu, LANES), lambda i: (0, i, 0, 0)),
            pl.BlockSpec((sources, orbs, nu, LANES), lambda i: (0, pairs // orbs, 0, 0)),
            pl.BlockSpec(other.shape, lambda i: (0, 0, 0, 0)),
        ],
        out_specs=pl.BlockSpec((HALF, SUBS * GROUP, sig), lambda i: (0, i, 0)),
        scratch_shapes=[
            pltpu.VMEM((orbs * LANES, sig), jnp.bfloat16),
            pltpu.VMEM((SUBS, orbs * HALF * PITCH, LANES), jnp.float32),
        ],
        compiler_params=pltpu.CompilerParams(vmem_limit_bytes=36 << 20),
        cost_estimate=pl.CostEstimate(
            flops=4 * HALF * pairs * orbs * LANES * sig, bytes_accessed=26 << 20, transcendentals=0
        ),
    )(pair_mask, aux_mask, moved, moved, other)


def local(three_centre, pair_mask, aux_mask, density):
    mu, nu, p_total = three_centre.shape
    aux_count, orbs = lax.axis_size("aux"), lax.axis_size("orb")
    own = density.T
    others = [lax.ppermute(own, "orb", [(i, i ^ step) for i in range(orbs)]) for step in range(1, orbs)]
    sent = pack(three_centre, orbs)
    sent = append(sent, (own, *others))
    moved = lax.all_to_all(sent, "aux", split_axis=0, concat_axis=0, tiled=True)
    other = lax.ppermute(moved[:, mu // 2 :], "aux", [(i, i ^ 1) for i in range(aux_count)])
    return contract(moved, other, pair_mask, aux_mask)


def solution(mesh):
    in_specs = (P("orb", "aux", None), P(), P(), P("orb", "aux"))
    out_specs = P("aux", "orb", None)
    return jax.shard_map(local, mesh=mesh, in_specs=in_specs, out_specs=out_specs, check_vma=False)
```

```python
import jax
import jax.numpy as jnp
from jax import lax
from jax.experimental import pallas as pl
from jax.experimental.pallas import tpu as pltpu
from jax.sharding import PartitionSpec as P

BLK = 128
LANES = 128
HALF = 64
GROUP = 16
PAIRS = 8
SUBS = 2
PITCH = 24


def pack_kernel(x_ref, o_ref, held_ref, sems):
    groups = x_ref.shape[0] // GROUP

    def fetch(group):
        rows = pl.ds(group * GROUP, GROUP)
        return pltpu.make_async_copy(x_ref.at[rows], held_ref.at[rows], sems.at[group])

    for group in range(groups):
        fetch(group).start()
    for group in range(groups):
        fetch(group).wait()
        top = group * GROUP
        for block in range(x_ref.shape[2] // LANES):
            lanes = slice(block * LANES, (block + 1) * LANES)
            low, high = held_ref[top : top + PAIRS, :, lanes], held_ref[top + PAIRS : top + GROUP, :, lanes]
            rows = slice(group * PAIRS, (group + 1) * PAIRS)
            o_ref[2 * block, rows] = jnp.concatenate([low[..., :HALF], high[..., :HALF]], axis=-1)
            o_ref[2 * block + 1, rows] = jnp.concatenate([low[..., HALF:], high[..., HALF:]], axis=-1)


def pack(three_centre, extra):
    mu, nu, p_total = three_centre.shape
    return pl.pallas_call(
        pack_kernel,
        out_shape=pltpu.VMEM((p_total // HALF, mu // 2 + extra, nu, LANES), jnp.bfloat16),
        in_specs=[pl.BlockSpec(memory_space=pl.ANY)],
        out_specs=pl.BlockSpec(memory_space=pltpu.VMEM),
        scratch_shapes=[pltpu.VMEM(three_centre.shape, jnp.bfloat16), pltpu.SemaphoreType.DMA((mu // GROUP,))],
        compiler_params=pltpu.CompilerParams(vmem_limit_bytes=36 << 20),
        cost_estimate=pl.CostEstimate(flops=0, bytes_accessed=4 * mu * nu * p_total, transcendentals=0),
    )(pltpu.with_memory_space_constraint(three_centre, pltpu.HBM))


def append_kernel(*refs):
    o_ref, parts = refs[-1], refs[:-2]
    half = parts[0].shape[0] // 2
    for step, part in enumerate(parts):
        orb = lax.axis_index("orb") ^ step
        for target in range(o_ref.shape[0]):
            core = target % 2
            o_ref[target, orb] = part[core * half : (core + 1) * half, :]


def append(sent, parts):
    targets, rows, nu, lanes = sent.shape
    orbs = len(parts)
    return pl.pallas_call(
        append_kernel,
        out_shape=jax.ShapeDtypeStruct(sent.shape, sent.dtype),
        grid=(1,),
        in_specs=[pl.BlockSpec(part.shape, lambda i: (0, 0)) for part in parts]
        + [pl.BlockSpec(memory_space=pl.ANY)],
        out_specs=pl.BlockSpec((targets, orbs, nu, lanes), lambda i: (0, rows // orbs - 1, 0, 0)),
        input_output_aliases={orbs: 0},
        compiler_params=pltpu.CompilerParams(vmem_limit_bytes=36 << 20),
    )(*parts, sent)


def contract_kernel(pair_ref, aux_ref, x_ref, other_ref, o_ref, dens_ref, rows_ref):
    sources, _, nu, _ = x_ref.shape
    depth = sources * nu
    _, orbs, half, lanes = other_ref.shape
    behind = x_ref.shape[1] - orbs
    first = pl.program_id(0) * SUBS * PAIRS
    aux_pos, orb_pos = lax.axis_index("aux"), lax.axis_index("orb")

    @pl.when(pl.program_id(0) == 0)
    def _():
        upper = lax.rem(aux_pos, 2) == 1
        column = lax.div(aux_pos * HALF, BLK)
        for orb in range(orbs):
            keep = (pair_ref[orb_pos, orb] * aux_ref[orb, column]).astype(jnp.float32).astype(jnp.bfloat16)
            mine, other = x_ref[:, behind + orb], other_ref[:, orb]
            low, high = jnp.where(upper, other, mine), jnp.where(upper, mine, other)
            whole = jnp.stack([low, high], axis=1).reshape(sources * 2 * half, lanes)
            dens_ref[orb * lanes : (orb + 1) * lanes, :] = whole.T * keep

    def order_rows(sub, pair):
        turned = x_ref[:, first + sub * PAIRS + pair].reshape(depth, LANES).T.astype(jnp.float32)
        for k in range(depth // LANES):
            piece = turned[:, k * LANES : (k + 1) * LANES]
            base = k * HALF * PITCH + pair
            rows_ref[sub, pl.ds(base, HALF, stride=PITCH), :] = piece[:HALF]
            rows_ref[sub, pl.ds(base + PAIRS, HALF, stride=PITCH), :] = piece[HALF:]

    def multiply(sub):
        pieces = []
        for k in range(depth // LANES):
            piece = rows_ref[sub, k * HALF * PITCH : (k + 1) * HALF * PITCH, :].reshape(HALF, PITCH, LANES)
            pieces.append(piece[:, :GROUP].reshape(HALF * GROUP, LANES).astype(jnp.bfloat16))
        product = jnp.dot(jnp.concatenate(pieces, axis=1), dens_ref[...], preferred_element_type=jnp.float32)
        mus = slice(sub * GROUP, (sub + 1) * GROUP)
        o_ref[:, mus] = product.astype(jnp.bfloat16).reshape(HALF, GROUP, -1)

    for sub in range(SUBS):
        for pair in range(PAIRS):
            order_rows(sub, pair)
    for sub in range(SUBS):
        multiply(sub)


def contract(moved, other, pair_mask, aux_mask):
    sources, orbs, nu, _ = other.shape
    pairs = moved.shape[1] - orbs
    sig = sources * 2 * nu
    return pl.pallas_call(
        contract_kernel,
        out_shape=jax.ShapeDtypeStruct((HALF, 2 * pairs, sig), jnp.bfloat16),
        grid=(pairs // (SUBS * PAIRS),),
        in_specs=[
            pl.BlockSpec(memory_space=pltpu.SMEM),
            pl.BlockSpec(memory_space=pltpu.SMEM),
            pl.BlockSpec(memory_space=pltpu.VMEM),
            pl.BlockSpec(other.shape, lambda i: (0, 0, 0, 0)),
        ],
        out_specs=pl.BlockSpec((HALF, SUBS * GROUP, sig), lambda i: (0, i, 0)),
        scratch_shapes=[
            pltpu.VMEM((orbs * LANES, sig), jnp.bfloat16),
            pltpu.VMEM((SUBS, orbs * HALF * PITCH, LANES), jnp.float32),
        ],
        compiler_params=pltpu.CompilerParams(vmem_limit_bytes=36 << 20),
        cost_estimate=pl.CostEstimate(
            flops=4 * HALF * pairs * orbs * LANES * sig, bytes_accessed=26 << 20, transcendentals=0
        ),
    )(pair_mask, aux_mask, pltpu.with_memory_space_constraint(moved, pltpu.VMEM), other)


def local(three_centre, pair_mask, aux_mask, density):
    mu, nu, p_total = three_centre.shape
    aux_count, orbs = lax.axis_size("aux"), lax.axis_size("orb")
    own = density.T
    others = [lax.ppermute(own, "orb", [(i, i ^ step) for i in range(orbs)]) for step in range(1, orbs)]
    sent = pack(three_centre, orbs)
    sent = append(sent, (own, *others))
    moved = lax.all_to_all(sent, "aux", split_axis=0, concat_axis=0, tiled=True)
    other = lax.ppermute(moved[:, mu // 2 :], "aux", [(i, i ^ 1) for i in range(aux_count)])
    return contract(moved, other, pair_mask, aux_mask)


def solution(mesh):
    in_specs = (P("orb", "aux", None), P(), P(), P("orb", "aux"))
    out_specs = P("aux", "orb", None)
    return jax.shard_map(local, mesh=mesh, in_specs=in_specs, out_specs=out_specs, check_vma=False)
```

```python
import jax
import jax.numpy as jnp
from jax import lax
from jax.experimental import pallas as pl
from jax.experimental.pallas import tpu as pltpu
from jax.sharding import PartitionSpec as P

BLK = 128
LANES = 128
HALF = 64
GROUP = 16
PAIRS = 8
SUBS = 1
PITCH = 24


def pack_kernel(x_ref, o_ref, held_ref, sems):
    groups = x_ref.shape[0] // GROUP

    def fetch(group):
        rows = pl.ds(group * GROUP, GROUP)
        return pltpu.make_async_copy(x_ref.at[rows], held_ref.at[rows], sems.at[group])

    for group in range(groups):
        fetch(group).start()
    for group in range(groups):
        fetch(group).wait()
        top = group * GROUP
        for block in range(x_ref.shape[2] // LANES):
            lanes = slice(block * LANES, (block + 1) * LANES)
            low, high = held_ref[top : top + PAIRS, :, lanes], held_ref[top + PAIRS : top + GROUP, :, lanes]
            rows = slice(group * PAIRS, (group + 1) * PAIRS)
            o_ref[2 * block, rows] = jnp.concatenate([low[..., :HALF], high[..., :HALF]], axis=-1)
            o_ref[2 * block + 1, rows] = jnp.concatenate([low[..., HALF:], high[..., HALF:]], axis=-1)


def pack(three_centre, extra):
    mu, nu, p_total = three_centre.shape
    return pl.pallas_call(
        pack_kernel,
        out_shape=pltpu.VMEM((p_total // HALF, mu // 2 + extra, nu, LANES), jnp.bfloat16),
        in_specs=[pl.BlockSpec(memory_space=pl.ANY)],
        out_specs=pl.BlockSpec(memory_space=pltpu.VMEM),
        scratch_shapes=[pltpu.VMEM(three_centre.shape, jnp.bfloat16), pltpu.SemaphoreType.DMA((mu // GROUP,))],
        compiler_params=pltpu.CompilerParams(vmem_limit_bytes=36 << 20),
        cost_estimate=pl.CostEstimate(flops=0, bytes_accessed=4 * mu * nu * p_total, transcendentals=0),
    )(pltpu.with_memory_space_constraint(three_centre, pltpu.HBM))


def append_kernel(*refs):
    o_ref, parts = refs[-1], refs[:-2]
    half = parts[0].shape[0] // 2
    for step, part in enumerate(parts):
        orb = lax.axis_index("orb") ^ step
        for target in range(o_ref.shape[0]):
            core = target % 2
            o_ref[target, orb] = part[core * half : (core + 1) * half, :]


def append(sent, parts):
    targets, rows, nu, lanes = sent.shape
    orbs = len(parts)
    return pl.pallas_call(
        append_kernel,
        out_shape=jax.ShapeDtypeStruct(sent.shape, sent.dtype),
        grid=(1,),
        in_specs=[pl.BlockSpec(part.shape, lambda i: (0, 0)) for part in parts]
        + [pl.BlockSpec(memory_space=pl.ANY)],
        out_specs=pl.BlockSpec((targets, orbs, nu, lanes), lambda i: (0, rows // orbs - 1, 0, 0)),
        input_output_aliases={orbs: 0},
        compiler_params=pltpu.CompilerParams(vmem_limit_bytes=36 << 20),
    )(*parts, sent)


def contract_kernel(pair_ref, aux_ref, x_ref, other_ref, o_ref, dens_ref, rows_ref):
    sources, _, nu, _ = x_ref.shape
    depth = sources * nu
    _, orbs, half, lanes = other_ref.shape
    behind = x_ref.shape[1] - orbs
    first = pl.program_id(0) * SUBS * PAIRS
    aux_pos, orb_pos = lax.axis_index("aux"), lax.axis_index("orb")

    @pl.when(pl.program_id(0) == 0)
    def _():
        upper = lax.rem(aux_pos, 2) == 1
        column = lax.div(aux_pos * HALF, BLK)
        for orb in range(orbs):
            keep = (pair_ref[orb_pos, orb] * aux_ref[orb, column]).astype(jnp.float32).astype(jnp.bfloat16)
            mine, other = x_ref[:, behind + orb], other_ref[:, orb]
            low, high = jnp.where(upper, other, mine), jnp.where(upper, mine, other)
            whole = jnp.stack([low, high], axis=1).reshape(sources * 2 * half, lanes)
            dens_ref[orb * lanes : (orb + 1) * lanes, :] = whole.T * keep

    def order_rows(sub, pair):
        turned = x_ref[:, first + sub * PAIRS + pair].reshape(depth, LANES).T.astype(jnp.float32)
        for k in range(depth // LANES):
            piece = turned[:, k * LANES : (k + 1) * LANES]
            base = k * HALF * PITCH + pair
            rows_ref[sub, pl.ds(base, HALF, stride=PITCH), :] = piece[:HALF]
            rows_ref[sub, pl.ds(base + PAIRS, HALF, stride=PITCH), :] = piece[HALF:]

    def multiply(sub):
        pieces = []
        for k in range(depth // LANES):
            piece = rows_ref[sub, k * HALF * PITCH : (k + 1) * HALF * PITCH, :].reshape(HALF, PITCH, LANES)
            pieces.append(piece[:, :GROUP].reshape(HALF * GROUP, LANES).astype(jnp.bfloat16))
        product = jnp.dot(jnp.concatenate(pieces, axis=1), dens_ref[...], preferred_element_type=jnp.float32)
        mus = slice(sub * GROUP, (sub + 1) * GROUP)
        o_ref[:, mus] = product.astype(jnp.bfloat16).reshape(HALF, GROUP, -1)

    for sub in range(SUBS):
        for pair in range(PAIRS):
            order_rows(sub, pair)
    for sub in range(SUBS):
        multiply(sub)


def contract(moved, other, pair_mask, aux_mask):
    sources, orbs, nu, _ = other.shape
    pairs = moved.shape[1] - orbs
    sig = sources * 2 * nu
    return pl.pallas_call(
        contract_kernel,
        out_shape=jax.ShapeDtypeStruct((HALF, 2 * pairs, sig), jnp.bfloat16),
        grid=(pairs // (SUBS * PAIRS),),
        in_specs=[
            pl.BlockSpec(memory_space=pltpu.SMEM),
            pl.BlockSpec(memory_space=pltpu.SMEM),
            pl.BlockSpec(memory_space=pltpu.VMEM),
            pl.BlockSpec(other.shape, lambda i: (0, 0, 0, 0)),
        ],
        out_specs=pl.BlockSpec((HALF, SUBS * GROUP, sig), lambda i: (0, i, 0)),
        scratch_shapes=[
            pltpu.VMEM((orbs * LANES, sig), jnp.bfloat16),
            pltpu.VMEM((SUBS, orbs * HALF * PITCH, LANES), jnp.float32),
        ],
        compiler_params=pltpu.CompilerParams(vmem_limit_bytes=36 << 20),
        cost_estimate=pl.CostEstimate(
            flops=4 * HALF * pairs * orbs * LANES * sig, bytes_accessed=26 << 20, transcendentals=0
        ),
    )(pair_mask, aux_mask, pltpu.with_memory_space_constraint(moved, pltpu.VMEM), other)


def local(three_centre, pair_mask, aux_mask, density):
    mu, nu, p_total = three_centre.shape
    aux_count, orbs = lax.axis_size("aux"), lax.axis_size("orb")
    own = density.T
    others = [lax.ppermute(own, "orb", [(i, i ^ step) for i in range(orbs)]) for step in range(1, orbs)]
    sent = pack(three_centre, orbs)
    sent = append(sent, (own, *others))
    moved = lax.all_to_all(sent, "aux", split_axis=0, concat_axis=0, tiled=True)
    other = lax.ppermute(moved[:, mu // 2 :], "aux", [(i, i ^ 1) for i in range(aux_count)])
    return contract(moved, other, pair_mask, aux_mask)


def solution(mesh):
    in_specs = (P("orb", "aux", None), P(), P(), P("orb", "aux"))
    out_specs = P("aux", "orb", None)
    return jax.shard_map(local, mesh=mesh, in_specs=in_specs, out_specs=out_specs, check_vma=False)
```
